512 devices in a mesh: dp: 32 (over y, x), tensor: 16 (over z, core).
Axes of the slice: x: 4, y: 8, z: 8, core: 2. Of those that a mesh axis runs over, the one named last changes fastest.
Arguments:
- grads: bfloat16 [16, 1024, 16384], P(None, 'dp', 'tensor')
- left_slot: int32 [16], replicated, may hold values from 0 to 15, each once
- left_roots: bfloat16 [16, 1024, 1024], P('tensor')
- right_roots: bfloat16 [16, 2048, 1024], P('tensor', 'dp')
Outputs:
- update: bfloat16 [16, 1024, 16384], P(None, 'dp', 'tensor')
The draws below stay inside these ranges and needn't reach their ends.
Inputs may be any that keep to these rules, and one draw needn't show every extreme that they name: left_slot names every stored left factor exactly once.
All inputs are finite; a program needn't handle non-finite values.
Results may differ from the reference program's by a relative error of at most 0.0049.
Values may be sent and summed in bfloat16 or wider, within the bound.
A program may use at most 64 MiB of HBM per device.

```python
import math
import jax
import jax.numpy as jnp
from jax import lax

B = 1024
MATS = 2
KR = 16
NBC = 16
COLS = 16384


def draw_grads(key, part):
    key = jax.random.fold_in(key, 11)
    key_rows, key_cols, key_values = jax.random.split(key, 3)
    total_rows = KR * B
    row_rough = jnp.exp(jax.random.uniform(key_rows, (total_rows, 1), jnp.float32, 0.0, math.log(10.0)))
    col_rough = jnp.exp(jax.random.uniform(key_cols, (1, COLS), jnp.float32, 0.0, math.log(10.0)))
    row_place = (jnp.arange(total_rows, dtype=jnp.int32) % B).astype(jnp.float32).reshape(total_rows, 1) / B
    col_place = (jnp.arange(COLS, dtype=jnp.int32) % B).astype(jnp.float32).reshape(1, COLS) / B
    row_scale = row_rough * jnp.exp(math.log(3.0) * row_place)
    col_scale = col_rough * jnp.exp(math.log(3.0) * col_place)
    values = jax.random.normal(key_values, (total_rows, COLS), jnp.float32)
    factor = 0.03
    return (values * row_scale * col_scale * factor).reshape(KR, B, COLS).astype(jnp.bfloat16)


def draw_left_roots(key, part):
    key = jax.random.fold_in(key, 23)
    key_diagonal, key_spread = jax.random.split(key)
    row_index = jnp.arange(B, dtype=jnp.int32).reshape(1, B, 1)
    col_index = jnp.arange(B, dtype=jnp.int32).reshape(1, 1, B)
    diagonal = jnp.exp(jax.random.uniform(key_diagonal, (KR, B, 1), jnp.float32, 0.0, math.log(10.0))) / 3.0
    spread = jax.random.normal(key_spread, (KR, B, B), jnp.float32) * 0.5
    return jnp.where(row_index == col_index, diagonal, spread * B ** (-0.5)).astype(jnp.bfloat16)


def draw_right_roots(key, part):
    key = jax.random.fold_in(key, 29)
    key_diagonal, key_spread = jax.random.split(key)
    row_index = jnp.arange(MATS * B, dtype=jnp.int32).reshape(1, MATS * B, 1) % B
    col_index = jnp.arange(B, dtype=jnp.int32).reshape(1, 1, B)
    diagonal = jnp.exp(jax.random.uniform(key_diagonal, (NBC, MATS * B, 1), jnp.float32, 0.0, math.log(10.0))) / 3.0
    spread = jax.random.normal(key_spread, (NBC, MATS * B, B), jnp.float32) * 0.5
    return jnp.where(row_index == col_index, diagonal, spread * B ** (-0.5)).astype(jnp.bfloat16)


def setup_inputs(seed: int = 0) -> dict:
    key_list = jax.random.split(jax.random.key(seed), 5)
    return {
        "grads": draw_grads(jax.random.fold_in(key_list[4], 71), 0),
        "left_slot": jax.random.permutation(key_list[1], KR).astype(jnp.int32),
        "left_roots": draw_left_roots(jax.random.fold_in(key_list[4], 71), 0),
        "right_roots": draw_right_roots(jax.random.fold_in(key_list[4], 71), 0),
    }


def reference(grads, left_slot, left_roots, right_roots):
    anchor = jnp.zeros((), jnp.int32)

    def one_block(flat_index):
        row_block = (flat_index // NBC).astype(jnp.int32)
        col_block = (flat_index % NBC).astype(jnp.int32)
        grad_block = lax.dynamic_slice(grads, (row_block, anchor, (col_block * B).astype(jnp.int32)), (1, B, B))[0]
        tile_slot = lax.dynamic_index_in_dim(left_slot, row_block, 0, keepdims=False).astype(jnp.int32)
        left_factor = lax.dynamic_index_in_dim(left_roots, tile_slot, 0, keepdims=False)
        matrix = (row_block % MATS).astype(jnp.int32)
        right_factor = lax.dynamic_slice(right_roots, (col_block, (matrix * B).astype(jnp.int32), anchor), (1, B, B))[0]
        mixed_part = jnp.dot(left_factor, grad_block, preferred_element_type=jnp.float32).astype(jnp.bfloat16)
        update_block = jnp.dot(mixed_part, right_factor, preferred_element_type=jnp.float32)
        grad_square = jnp.sum(jnp.square(grad_block.astype(jnp.float32)))
        update_square = jnp.sum(update_block * update_block)
        return (update_block * jnp.sqrt(grad_square / (update_square + 1e-06))).astype(jnp.bfloat16)
    blocks = lax.map(one_block, jnp.arange(KR * NBC, dtype=jnp.int32))
    blocks = blocks.reshape(KR, NBC, B, B)
    return jnp.swapaxes(blocks, 1, 2).reshape(KR, B, NBC * B)
```

```python
import functools

import jax
import jax.numpy as jnp
from jax import lax
from jax.experimental import pallas as pl
from jax.experimental.pallas import tpu as pltpu
from jax.sharding import PartitionSpec as P

MESH = pl.DeviceIdType.MESH
CHIPS_X = 4
MATS = 2
MIB = 1 << 20


def kernel(
    nx, ny, nz, chunks,
    slot_ref, g_ref, p_ref, q_ref, o_ref,
    g_stage, g_full, p_half, q_relay, q_stage, q_full, z_buf, u_buf, u_stage, u_recv, sums, sums_in,
    g_send, g_recv, gf_send, gf_recv, p_send, p_sib, p_recv, q_send, q_recv, x_send, x_recv,
    qf_send, qf_recv, s_sem, u_send, u_in,
):
    half = ny // 2
    fold = half // 2
    slots = half * nx
    rows = g_ref.shape[1]
    block = g_ref.shape[2]
    half_block = block // 2
    part = half_block // chunks
    dp = lax.axis_index("dp")
    tensor = lax.axis_index("tensor")
    y, x = dp // nx, dp % nx
    z, core = tensor // 2, tensor % 2
    side, y_low = y // half, y % half
    mine = y_low * nx + x
    own = core == side
    sibling = (dp, z * 2 + 1 - core)
    step = 1 - 2 * core
    z_next = (dp, ((z + step + nz) % nz) * 2 + core)
    z_prev = (dp, ((z - step + nz) % nz) * 2 + core)
    hop = ((z - mine // 2) * step + nz) % nz
    source = (hop == 0) & (core == mine % 2)
    q_core = y_low // fold
    q_own = own & (q_core == core)

    def inverse(slot):
        found = 0
        for k in range(slots):
            found = jnp.where(slot_ref[k] == slot, k, found)
        return found

    def place(offset, sign):
        py = (y_low + sign * (offset // nx) + half) % half
        px = (x + sign * (offset % nx) + nx) % nx
        return py * nx + px

    def partner(pos):
        return (core * slots + pos, z * 2 + side)

    def remote(src, dst, send, recv, device):
        return pltpu.make_async_remote_copy(
            src_ref=src, dst_ref=dst, send_sem=send, recv_sem=recv, device_id=device, device_id_type=MESH
        )

    def arrived(dst, sem):
        pltpu.make_async_copy(dst, dst, sem).wait()

    def g_rows(which, pos):
        return g_full.at[pl.ds(pl.multiple_of((which * slots + pos) * rows, rows), rows), :]

    barrier = pltpu.get_barrier_semaphore()

    def greet(device):
        pl.semaphore_signal(barrier, inc=1, device_id=device, device_id_type=MESH)

    @pl.loop(1, slots)
    def _(offset):
        greet(partner(place(offset, 1)))

    @pl.when(jnp.logical_not(own))
    def _():
        greet(partner(mine))

    @pl.loop(0, half)
    def _(i):
        py = (i // fold) * half + core * fold + i % fold

        @pl.when(jnp.logical_not(q_own & (py == y)))
        def _():
            greet((py * nx + x, z * 2 + side))

    @pl.loop(1, nx)
    def _(ox):
        greet((y * nx + (x + ox) % nx, tensor))

    greet(sibling)
    greet(z_prev)

    @pl.loop(0, slots)
    def _(offset):
        g_stage[offset] = g_ref[inverse(place(offset, 1))]

    pl.semaphore_wait(
        barrier,
        slots - own.astype(jnp.int32) + half - q_own.astype(jnp.int32) + nx - 1 + 2,
    )

    def q_out(i):
        return remote(
            q_ref.at[0], q_relay.at[side, y_low % fold], q_send.at[i], q_recv.at[side, y_low % fold],
            ((core * half + i) * nx + x, z * 2 + q_core),
        )

    @pl.loop(0, half)
    def _(j):
        i = (y_low + j) % half
        keep = q_own & (i == y_low)

        @pl.when(keep)
        def _():
            pltpu.make_async_copy(
                q_ref.at[0], q_relay.at[side, y_low % fold], q_recv.at[side, y_low % fold]
            ).start()

        @pl.when(jnp.logical_not(keep))
        def _():
            q_out(i).start()

    def p_part(t):
        return p_half.at[pl.ds(pl.multiple_of(t * part, part), part), :]

    def p_stored(which, t):
        return p_ref.at[0, pl.ds(pl.multiple_of(which * half_block + t * part, part), part), :]

    def p_side(t):
        return remote(p_stored(1 - core, t), p_part(t), p_sib.at[t], p_recv.at[t], sibling)

    def p_out(t):
        return remote(p_part(t), p_part(t), p_send.at[t], p_recv.at[t], z_next)

    @pl.when(source)
    def _():
        @pl.loop(0, chunks)
        def _(t):
            pltpu.make_async_copy(p_stored(core, t), p_part(t), p_recv.at[t]).start()
            p_side(t).start()

    def g_out(offset):
        return remote(
            g_stage.at[offset], g_rows(side, mine), g_send.at[offset], g_recv.at[offset],
            partner(place(offset, 1)),
        )

    @pl.when(own)
    def _():
        pltpu.make_async_copy(g_stage.at[0], g_rows(side, mine), g_recv.at[0]).start()

    @pl.when(jnp.logical_not(own))
    def _():
        g_out(0).start()

    @pl.loop(1, slots)
    def _(offset):
        g_out(offset).start()

    @pl.loop(0, half)
    def _(i):
        arrived(q_relay.at[i // fold, i % fold], q_recv.at[i // fold, i % fold])

    def x_out(ox):
        return remote(
            q_stage.at[ox], q_full.at[core, :, x], x_send.at[ox], x_recv.at[ox], (y * nx + (x + ox) % nx, tensor)
        )

    @pl.loop(1, nx)
    def _(ox):
        q_stage[ox] = q_relay[inverse(y_low * nx + (x + ox) % nx) % MATS]
        x_out(ox).start()

    q_full[core, :, x] = q_relay[inverse(mine) % MATS]

    def q_forward(ox):
        piece = q_full.at[core, :, (x - ox + nx) % nx]
        return remote(piece, piece, qf_send.at[ox], qf_recv.at[ox], sibling)

    q_forward(0).start()

    def g_forward(offset):
        piece = g_rows(core, place(offset, -1))
        return remote(piece, piece, gf_send.at[offset], gf_recv.at[offset], sibling)

    steps = max(chunks, slots)

    def pass_on(t, total):
        if chunks == steps:
            arrived(p_part(t), p_recv.at[t])

            @pl.when(hop < nz - 1)
            def _():
                p_out(t).start()

        pos = place(t, -1)
        arrived(g_rows(core, pos), g_recv.at[t])
        g_forward(t).start()
        values = g_rows(core, pos)[...].astype(jnp.float32)
        return total + jnp.sum((values * values).reshape(-1, 8, 128), axis=0)

    sums[0] = lax.fori_loop(0, slots, pass_on, jnp.zeros((8, 128), jnp.float32))

    @pl.loop(1, nx)
    def _(ox):
        arrived(q_full.at[core, :, (x - ox + nx) % nx], x_recv.at[ox])
        q_forward(ox).start()

    @pl.loop(0, slots)
    def _(offset):
        arrived(g_rows(1 - core, place(offset, -1)), gf_recv.at[offset])

    width = 256

    @pl.loop(0, block // width)
    def _(n):
        cols = pl.ds(pl.multiple_of(n * width, width), width)
        z_buf[:, cols] = jnp.dot(p_half[...], g_full[:, cols], preferred_element_type=jnp.float32).astype(
            jnp.bfloat16
        )

    @pl.loop(0, nx)
    def _(ox):
        arrived(q_full.at[1 - core, :, (x - ox + nx) % nx], qf_recv.at[ox])

    def right(n, total):
        cols = pl.ds(pl.multiple_of(n * width, width), width)
        factor = q_full[:, :, :, :, cols].reshape(block, width)
        value = jnp.dot(z_buf[...], factor, preferred_element_type=jnp.float32)
        u_buf[:, cols] = value
        return total + jnp.sum((value * value).reshape(-1, 8, 128), axis=0)

    sums[1] = lax.fori_loop(0, block // width, right, jnp.zeros((8, 128), jnp.float32))

    exchange = remote(sums, sums_in, s_sem.at[0], s_sem.at[1], sibling)
    exchange.start()
    exchange.wait()
    graft = jnp.sqrt(jnp.sum(sums[0] + sums_in[0]) / (jnp.sum(sums[1] + sums_in[1]) + 1e-06))

    def u_out(offset):
        return remote(
            u_stage.at[offset], u_recv.at[mine], u_send.at[offset], u_in.at[offset],
            partner(place(offset, -1)),
        )

    def u_scaled(offset):
        first = pl.multiple_of(place(offset, -1) * rows, rows)
        return (u_buf[pl.ds(first, rows), :] * graft).astype(jnp.bfloat16)

    u_stage[0] = u_scaled(0)

    @pl.when(own)
    def _():
        pltpu.make_async_copy(u_stage.at[0], u_recv.at[mine], u_in.at[0]).start()

    @pl.when(jnp.logical_not(own))
    def _():
        u_out(0).start()

    @pl.loop(1, slots)
    def _(offset):
        u_stage[offset] = u_scaled(offset)
        u_out(offset).start()

    @pl.when(jnp.logical_not(own))
    def _():
        g_out(0).wait_send()

    @pl.loop(1, slots)
    def _(offset):
        g_out(offset).wait_send()

    @pl.loop(0, half)
    def _(i):
        @pl.when(jnp.logical_not(q_own & (i == y_low)))
        def _():
            q_out(i).wait_send()

    @pl.loop(1, nx)
    def _(ox):
        x_out(ox).wait_send()

    @pl.loop(0, nx)
    def _(ox):
        q_forward(ox).wait_send()

    @pl.loop(0, slots)
    def _(offset):
        g_forward(offset).wait_send()

    @pl.when(source)
    def _():
        @pl.loop(0, chunks)
        def _(t):
            p_side(t).wait_send()

    @pl.when(hop < nz - 1)
    def _():
        @pl.loop(0, chunks)
        def _(t):
            p_out(t).wait_send()

    @pl.loop(0, slots)
    def _(offset):
        arrived(u_recv.at[place(offset, 1)], u_in.at[offset])

    @pl.when(jnp.logical_not(own))
    def _():
        u_out(0).wait_send()

    @pl.loop(1, slots)
    def _(offset):
        u_out(offset).wait_send()

    @pl.loop(0, slots)
    def _(k):
        o_ref[k] = u_recv[slot_ref[k]]


def local(nx, ny, nz, grads, left_slot, left_roots, right_roots):
    slots, rows, block = grads.shape
    half = ny // 2
    fold = half // 2
    chunks = slots
    shard = right_roots.shape[1]
    bf16, f32 = jnp.bfloat16, jnp.float32
    dma = pltpu.SemaphoreType.DMA
    vmem = pl.BlockSpec(memory_space=pltpu.VMEM)
    anywhere = pl.BlockSpec(memory_space=pl.ANY)
    return pl.pallas_call(
        functools.partial(kernel, nx, ny, nz, chunks),
        out_shape=jax.ShapeDtypeStruct(grads.shape, bf16),
        in_specs=[pl.BlockSpec(memory_space=pltpu.SMEM), vmem, anywhere, anywhere],
        out_specs=vmem,
        scratch_shapes=[
            pltpu.VMEM((slots, rows, block), bf16),
            pltpu.VMEM((block, block), bf16),
            pltpu.VMEM((block // 2, block), bf16),
            pltpu.VMEM((MATS, fold, shard, block), bf16),
            pltpu.VMEM((nx, fold, shard, block), bf16),
            pltpu.VMEM((2, fold, nx, shard, block), bf16),
            pltpu.VMEM((block // 2, block), bf16),
            pltpu.VMEM((block // 2, block), f32),
            pltpu.VMEM((slots, rows, block), bf16),
            pltpu.VMEM((slots, rows, block), bf16),
            pltpu.VMEM((2, 8, 128), f32),
            pltpu.VMEM((2, 8, 128), f32),
            dma((slots,)), dma((slots,)), dma((slots,)), dma((slots,)),
            dma((chunks,)), dma((chunks,)), dma((chunks,)),
            dma((half,)), dma((MATS, fold)),
            dma((nx,)), dma((nx,)), dma((nx,)), dma((nx,)),
            dma((2,)),
            dma((slots,)), dma((slots,)),
        ],
        compiler_params=pltpu.CompilerParams(
            collective_id=0, has_side_effects=True, vmem_limit_bytes=40 * MIB
        ),
        cost_estimate=pl.CostEstimate(
            flops=2 * block * block * block, bytes_accessed=16 * MIB, transcendentals=0
        ),
        name="precondition",
    )(left_slot, grads, left_roots, right_roots)


def solution(mesh):
    nx = CHIPS_X
    ny = mesh.shape["dp"] // nx
    nz = mesh.shape["tensor"] // 2
    in_specs = (P(None, "dp", "tensor"), P(), P("tensor", None, None), P("tensor", "dp", None))
    out_specs = P(None, "dp", "tensor")
    return jax.shard_map(
        functools.partial(local, nx, ny, nz), mesh=mesh, in_specs=in_specs, out_specs=out_specs, check_vma=False
    )
```

```python
import functools

import jax
import jax.numpy as jnp
from jax import lax
from jax.experimental import pallas as pl
from jax.experimental.pallas import tpu as pltpu
from jax.sharding import PartitionSpec as P

MESH = pl.DeviceIdType.MESH
CHIPS_X = 4
MATS = 2
MIB = 1 << 20
PIECES = 2


def kernel(
    nx, ny, nz, chunks,
    slot_ref, g_hbm, p_ref, q_ref, o_ref,
    g_ref, g_stage, g_full, p_half, q_relay_first, q_relay_last, q_stage, q_full, z_sum, z_buf, u_buf, u_stage, u_recv, sums, sums_in,
    g_send, g_recv, gf_send, gf_recv, p_send, p_sib, p_recv, q_send, q_recv, x_send, x_recv,
    qf_send, qf_recv, s_sem, u_send, u_in, in_sem,
):
    half = ny // 2
    fold = half // 2
    slots = half * nx
    rows = g_ref.shape[1]
    block = g_ref.shape[2]
    half_block = block // 2
    part = half_block // chunks
    dp = lax.axis_index("dp")
    tensor = lax.axis_index("tensor")
    y, x = dp // nx, dp % nx
    z, core = tensor // 2, tensor % 2
    side, y_low = y // half, y % half
    mine = y_low * nx + x
    own = core == side
    sibling = (dp, z * 2 + 1 - core)
    step = 1 - 2 * core
    z_next = (dp, ((z + step + nz) % nz) * 2 + core)
    z_prev = (dp, ((z - step + nz) % nz) * 2 + core)
    hop = ((z - mine // 2) * step + nz) % nz
    source = (hop == 0) & (core == mine % 2)
    q_core = y_low // fold
    q_own = own & (q_core == core)

    def inverse(slot):
        found = 0
        for k in range(slots):
            found = jnp.where(slot_ref[k] == slot, k, found)
        return found

    def place(offset, sign):
        py = (y_low + sign * (offset // nx) + half) % half
        px = (x + sign * (offset % nx) + nx) % nx
        return py * nx + px

    pairs = nx // 2
    wave_size = slots // 2

    def target(w):
        wave, i = w // wave_size, w % wave_size
        py = (y_low + i // pairs) % half
        px = 2 * ((x // 2 + i) % pairs) + (wave + py) % 2
        return py * nx + px

    def sender(e):
        i = e // 2
        sy = (y_low - i // pairs + half) % half
        sx = 2 * ((x // 2 - i % pairs + pairs) % pairs) + e % 2
        return sy * nx + sx

    def partner(pos):
        return (core * slots + pos, z * 2 + side)

    def remote(src, dst, send, recv, device):
        return pltpu.make_async_remote_copy(
            src_ref=src, dst_ref=dst, send_sem=send, recv_sem=recv, device_id=device, device_id_type=MESH
        )

    def arrived(dst, sem):
        pltpu.make_async_copy(dst, dst, sem).wait()

    def g_rows(which, pos):
        return g_full.at[pl.ds(pl.multiple_of((which * slots + pos) * rows, rows), rows), :]

    own_rows = pltpu.make_async_copy(g_hbm, g_ref, in_sem)
    own_rows.start()

    barrier = pltpu.get_barrier_semaphore()

    def greet(device):
        pl.semaphore_signal(barrier, inc=1, device_id=device, device_id_type=MESH)

    @pl.loop(1, slots)
    def _(offset):
        greet(partner(place(offset, 1)))

    @pl.when(jnp.logical_not(own))
    def _():
        greet(partner(mine))

    @pl.loop(0, half)
    def _(i):
        py = (i // fold) * half + core * fold + i % fold

        @pl.when(jnp.logical_not(q_own & (py == y)))
        def _():
            greet((py * nx + x, z * 2 + side))

    @pl.loop(1, nx)
    def _(ox):
        greet((y * nx + (x + ox) % nx, tensor))

    greet(sibling)
    greet(z_prev)

    own_rows.wait()

    @pl.loop(0, slots)
    def _(offset):
        g_stage[offset] = g_ref[inverse(target(offset))]

    pl.semaphore_wait(
        barrier,
        slots - own.astype(jnp.int32) + half - q_own.astype(jnp.int32) + nx - 1 + 2,
    )

    shard = q_ref.shape[1]
    pieces = PIECES
    piece = shard // pieces
    q_relay = (q_relay_first, q_relay_last)

    def q_span(part):
        return pl.ds(part * piece, piece)

    def q_spot(hh, i, part):
        return q_relay[part].at[hh, i]

    def q_out(i, part):
        return remote(
            q_ref.at[0, q_span(part)], q_spot(side, y_low % fold, part), q_send.at[i, part],
            q_recv.at[side, y_low % fold, part], ((core * half + i) * nx + x, z * 2 + q_core),
        )

    def send_q():
        for part in range(pieces):

            @pl.loop(0, half)
            def _(j):
                i = (y_low + j) % half
                keep = q_own & (i == y_low)

                @pl.when(keep)
                def _():
                    pltpu.make_async_copy(
                        q_ref.at[0, q_span(part)], q_spot(side, y_low % fold, part),
                        q_recv.at[side, y_low % fold, part],
                    ).start()

                @pl.when(jnp.logical_not(keep))
                def _():
                    q_out(i, part).start()

    def p_part(t):
        return p_half.at[pl.ds(pl.multiple_of(t * part, part), part), :]

    def p_stored(which, t):
        return p_ref.at[0, pl.ds(pl.multiple_of(which * half_block + t * part, part), part), :]

    def p_side(t):
        return remote(p_stored(1 - core, t), p_part(t), p_sib.at[t], p_recv.at[t], sibling)

    def p_out(t):
        return remote(p_part(t), p_part(t), p_send.at[t], p_recv.at[t], z_next)

    def p_first(t):
        return remote(p_stored(core, t), p_part(t), p_send.at[t], p_recv.at[t], z_next)

    passes = (hop < nz - 1) & jnp.logical_not(source)

    def send_p():
        @pl.when(source)
        def _():
            @pl.loop(0, chunks)
            def _(t):
                p_first(t).start()
                p_side(t).start()
                pltpu.make_async_copy(p_stored(core, t), p_part(t), p_recv.at[t]).start()

    def pass_p(first, last):
        @pl.loop(first, last)
        def _(t):
            arrived(p_part(t), p_recv.at[t])

            @pl.when(passes)
            def _():
                p_out(t).start()

    def g_out(w):
        return remote(
            g_stage.at[w], g_rows(side, mine), g_send.at[w], g_recv.at[2 * (w % wave_size) + x % 2],
            partner(target(w)),
        )

    def send_g(first, last):
        @pl.loop(first, last)
        def _(w):
            keep = own & (target(w) == mine)

            @pl.when(keep)
            def _():
                pltpu.make_async_copy(g_stage.at[w], g_rows(side, mine), g_recv.at[x % 2]).start()

            @pl.when(jnp.logical_not(keep))
            def _():
                g_out(w).start()

    def q_part(which, column, part):
        return q_full.at[which, :, column, q_span(part)]

    def x_out(ox, part):
        return remote(
            q_stage.at[ox, :, q_span(part)], q_part(core, x, part), x_send.at[ox, part], x_recv.at[ox, part],
            (y * nx + (x + ox) % nx, tensor),
        )

    def q_forward(ox, part):
        spot = q_part(core, (x - ox + nx) % nx, part)
        return remote(spot, spot, qf_send.at[ox, part], qf_recv.at[ox, part], sibling)

    def turn_q(part):
        @pl.loop(0, half)
        def _(i):
            arrived(q_spot(i // fold, i % fold, part), q_recv.at[i // fold, i % fold, part])

        @pl.loop(1, nx)
        def _(ox):
            q_stage[ox, :, q_span(part)] = q_relay[part][inverse(y_low * nx + (x + ox) % nx) % MATS]
            x_out(ox, part).start()

        q_full[core, :, x, q_span(part)] = q_relay[part][inverse(mine) % MATS]
        q_forward(0, part).start()

    def pass_q():
        for part in range(pieces):

            @pl.loop(1, nx)
            def _(ox):
                arrived(q_part(core, (x - ox + nx) % nx, part), x_recv.at[ox, part])
                q_forward(ox, part).start()

    def take_q():
        for part in range(pieces):

            @pl.loop(0, nx)
            def _(ox):
                arrived(q_part(1 - core, (x - ox + nx) % nx, part), qf_recv.at[ox, part])

    def g_forward(offset):
        piece = g_rows(core, sender(offset))
        return remote(piece, piece, gf_send.at[offset], gf_recv.at[offset], sibling)

    def pass_g(first, last, total):
        def one(t, total):
            pos = sender(t)
            arrived(g_rows(core, pos), g_recv.at[t])
            g_forward(t).start()
            values = g_rows(core, pos)[...].astype(jnp.float32)
            return total + jnp.sum((values * values).reshape(-1, 8, 128), axis=0)

        return lax.fori_loop(first, last, one, total)

    def take_g(first, last):
        @pl.loop(first, last)
        def _(offset):
            arrived(g_rows(1 - core, sender(offset)), gf_recv.at[offset])

    width = 256

    span = rows * nx

    def left_part(which, first, begin, end):
        tops = [
            pl.multiple_of((which * slots + ((y_low - first - i + half) % half) * nx) * rows, span) for i in range(2)
        ]
        left = jnp.concatenate([p_half[:, pl.ds(top, span)] for top in tops], axis=1)

        @pl.loop(0, block // width)
        def _(n):
            cols = pl.ds(pl.multiple_of(n * width, width), width)
            right = jnp.concatenate([g_full[pl.ds(top, span), cols] for top in tops], axis=0)
            value = jnp.dot(left, right, preferred_element_type=jnp.float32)
            if not begin:
                value = z_sum[:, cols] + value
            if end:
                z_buf[:, cols] = value.astype(jnp.bfloat16)
            else:
                z_sum[:, cols] = value

    def right_product():
        def right(n, total):
            cols = pl.ds(pl.multiple_of(n * width, width), width)
            factor = q_full[:, :, :, :, cols].reshape(block, width)
            value = jnp.dot(z_buf[...], factor, preferred_element_type=jnp.float32)
            u_buf[:, cols] = value
            return total + jnp.sum((value * value).reshape(-1, 8, 128), axis=0)

        return lax.fori_loop(0, block // width, right, jnp.zeros((8, 128), jnp.float32))

    def u_out(offset):
        return remote(
            u_stage.at[offset], u_recv.at[mine], u_send.at[offset], u_in.at[offset],
            partner(place(offset, -1)),
        )

    def send_u(graft):
        def scaled(offset):
            first = pl.multiple_of(place(offset, -1) * rows, rows)
            return (u_buf[pl.ds(first, rows), :] * graft).astype(jnp.bfloat16)

        u_stage[0] = scaled(0)

        @pl.when(own)
        def _():
            pltpu.make_async_copy(u_stage.at[0], u_recv.at[mine], u_in.at[0]).start()

        @pl.when(jnp.logical_not(own))
        def _():
            u_out(0).start()

        @pl.loop(1, slots)
        def _(offset):
            u_stage[offset] = scaled(offset)
            u_out(offset).start()

    def sent_g(first, last):
        @pl.loop(first, last)
        def _(w):
            @pl.when(jnp.logical_not(own & (target(w) == mine)))
            def _():
                g_out(w).wait_send()

    def left_g():
        @pl.loop(0, slots)
        def _(offset):
            g_forward(offset).wait_send()

    def left_q():
        for part in range(pieces):

            @pl.loop(0, half)
            def _(i):
                @pl.when(jnp.logical_not(q_own & (i == y_low)))
                def _():
                    q_out(i, part).wait_send()

            @pl.loop(1, nx)
            def _(ox):
                x_out(ox, part).wait_send()

            @pl.loop(0, nx)
            def _(ox):
                q_forward(ox, part).wait_send()

    def left_p():
        @pl.when(source)
        def _():
            @pl.loop(0, chunks)
            def _(t):
                p_side(t).wait_send()

        @pl.when(hop < nz - 1)
        def _():
            @pl.loop(0, chunks)
            def _(t):
                p_out(t).wait_send()

    def take_u():
        @pl.loop(0, slots)
        def _(offset):
            arrived(u_recv.at[place(offset, 1)], u_in.at[offset])

        @pl.when(jnp.logical_not(own))
        def _():
            u_out(0).wait_send()

        @pl.loop(1, slots)
        def _(offset):
            u_out(offset).wait_send()

    send_q()
    send_p()
    send_g(0, wave_size // 2)
    first_cut = jnp.clip((9 - 3 * hop) * 4 // 3 * chunks // 16, 0, chunks)
    second_cut = jnp.clip((15 - 3 * hop) * 4 // 3 * chunks // 16, first_cut, chunks)
    pass_p(0, first_cut)
    turn_q(0)
    send_g(wave_size // 2, wave_size)
    pass_p(first_cut, second_cut)
    turn_q(1)
    send_g(wave_size, slots)
    pass_p(second_cut, chunks)
    zero = jnp.zeros((8, 128), jnp.float32)
    pass_q()
    middle = slots // 2
    part_sum = pass_g(0, middle, zero)
    left_part(core, 0, True, False)
    take_g(0, middle)
    left_part(1 - core, 0, False, False)
    sums[0] = pass_g(middle, slots, part_sum)
    left_part(core, 2, False, False)
    take_g(middle, slots)
    left_part(1 - core, 2, False, True)
    take_q()
    sums[1] = right_product()
    exchange = remote(sums, sums_in, s_sem.at[0], s_sem.at[1], sibling)
    exchange.start()
    exchange.wait()
    graft = jnp.sqrt(jnp.sum(sums[0] + sums_in[0]) / (jnp.sum(sums[1] + sums_in[1]) + 1e-06))
    send_u(graft)
    sent_g(0, slots)
    left_g()
    left_q()
    left_p()
    take_u()

    @pl.loop(0, slots)
    def _(k):
        o_ref[k] = u_recv[slot_ref[k]]


def local(nx, ny, nz, grads, left_slot, left_roots, right_roots):
    slots, rows, block = grads.shape
    half = ny // 2
    fold = half // 2
    chunks = slots
    pieces = PIECES
    shard = right_roots.shape[1]
    bf16, f32 = jnp.bfloat16, jnp.float32
    dma = pltpu.SemaphoreType.DMA
    vmem = pl.BlockSpec(memory_space=pltpu.VMEM)
    hbm = pl.BlockSpec(memory_space=pl.ANY)
    return pl.pallas_call(
        functools.partial(kernel, nx, ny, nz, chunks),
        out_shape=jax.ShapeDtypeStruct(grads.shape, bf16),
        in_specs=[pl.BlockSpec(memory_space=pltpu.SMEM), hbm, hbm, hbm],
        out_specs=vmem,
        scratch_shapes=[
            pltpu.VMEM((slots, rows, block), bf16),
            pltpu.VMEM((slots, rows, block), bf16),
            pltpu.VMEM((block, block), bf16),
            pltpu.VMEM((block // 2, block), bf16),
            pltpu.VMEM((MATS, fold, shard // pieces, block), bf16),
            pltpu.VMEM((MATS, fold, shard // pieces, block), bf16),
            pltpu.VMEM((nx, fold, shard, block), bf16),
            pltpu.VMEM((2, fold, nx, shard, block), bf16),
            pltpu.VMEM((block // 2, block), f32),
            pltpu.VMEM((block // 2, block), bf16),
            pltpu.VMEM((block // 2, block), f32),
            pltpu.VMEM((slots, rows, block), bf16),
            pltpu.VMEM((slots, rows, block), bf16),
            pltpu.VMEM((2, 8, 128), f32),
            pltpu.VMEM((2, 8, 128), f32),
            dma((slots,)), dma((slots,)), dma((slots,)), dma((slots,)),
            dma((chunks,)), dma((chunks,)), dma((chunks,)),
            dma((half, pieces)), dma((MATS, fold, pieces)),
            dma((nx, pieces)), dma((nx, pieces)), dma((nx, pieces)), dma((nx, pieces)),
            dma((2,)),
            dma((slots,)), dma((slots,)), dma,
        ],
        compiler_params=pltpu.CompilerParams(
            collective_id=0, has_side_effects=True, vmem_limit_bytes=60 * MIB
        ),
        cost_estimate=pl.CostEstimate(
            flops=2 * block * block * block, bytes_accessed=16 * MIB, transcendentals=0
        ),
        name="precondition",
    )(left_slot, grads, left_roots, right_roots)


def solution(mesh):
    nx = CHIPS_X
    ny = mesh.shape["dp"] // nx
    nz = mesh.shape["tensor"] // 2
    in_specs = (P(None, "dp", "tensor"), P(), P("tensor", None, None), P("tensor", "dp", None))
    out_specs = P(None, "dp", "tensor")
    return jax.shard_map(
        functools.partial(local, nx, ny, nz), mesh=mesh, in_specs=in_specs, out_specs=out_specs, check_vma=False
    )
```

```python
import functools

import jax
import jax.numpy as jnp
from jax import lax
from jax.experimental import pallas as pl
from jax.experimental.pallas import tpu as pltpu
from jax.sharding import PartitionSpec as P

MESH = pl.DeviceIdType.MESH
CHIPS_X = 4
MATS = 2
MIB = 1 << 20
PIECES = 2


def kernel(
    nx, ny, nz, chunks,
    slot_ref, g_hbm, p_ref, q_ref, o_ref,
    g_ref, g_stage, g_full, p_half, q_relay_first, q_relay_last, q_stage, q_full, z_sum, z_buf, u_buf, u_stage, u_recv, sums, sums_in,
    g_send, g_recv, gf_send, gf_recv, p_send, p_sib, p_recv, q_send, q_recv, x_send, x_recv,
    qf_send, qf_recv, s_sem, u_send, u_in, in_sem,
):
    half = ny // 2
    fold = half // 2
    slots = half * nx
    rows = g_ref.shape[1]
    block = g_ref.shape[2]
    half_block = block // 2
    part = half_block // chunks
    dp = lax.axis_index("dp")
    tensor = lax.axis_index("tensor")
    y, x = dp // nx, dp % nx
    z, core = tensor // 2, tensor % 2
    side, y_low = y // half, y % half
    mine = y_low * nx + x
    own = core == side
    sibling = (dp, z * 2 + 1 - core)
    step = 1 - 2 * core
    z_next = (dp, ((z + step + nz) % nz) * 2 + core)
    z_prev = (dp, ((z - step + nz) % nz) * 2 + core)
    hop = ((z - mine // 2) * step + nz) % nz
    source = (hop == 0) & (core == mine % 2)
    q_core = y_low // fold
    q_own = own & (q_core == core)

    def inverse(slot):
        found = 0
        for k in range(slots):
            found = jnp.where(slot_ref[k] == slot, k, found)
        return found

    def place(offset, sign):
        py = (y_low + sign * (offset // nx) + half) % half
        px = (x + sign * (offset % nx) + nx) % nx
        return py * nx + px

    pairs = nx // 2
    wave_size = slots // 2

    def target(w):
        wave, i = w // wave_size, w % wave_size
        py = (y_low + i // pairs) % half
        px = 2 * ((x // 2 + i) % pairs) + (wave + py) % 2
        return py * nx + px

    def sender(e):
        i = e // 2
        sy = (y_low - i // pairs + half) % half
        sx = 2 * ((x // 2 - i % pairs + pairs) % pairs) + e % 2
        return sy * nx + sx

    def partner(pos):
        return (core * slots + pos, z * 2 + side)

    def remote(src, dst, send, recv, device):
        return pltpu.make_async_remote_copy(
            src_ref=src, dst_ref=dst, send_sem=send, recv_sem=recv, device_id=device, device_id_type=MESH
        )

    def arrived(dst, sem):
        pltpu.make_async_copy(dst, dst, sem).wait()

    def g_rows(which, pos):
        return g_full.at[pl.ds(pl.multiple_of((which * slots + pos) * rows, rows), rows), :]

    own_rows = pltpu.make_async_copy(g_hbm, g_ref, in_sem)
    own_rows.start()

    barrier = pltpu.get_barrier_semaphore()

    def greet(device):
        pl.semaphore_signal(barrier, inc=1, device_id=device, device_id_type=MESH)

    @pl.loop(1, slots)
    def _(offset):
        greet(partner(place(offset, 1)))

    @pl.when(jnp.logical_not(own))
    def _():
        greet(partner(mine))

    @pl.loop(0, half)
    def _(i):
        py = (i // fold) * half + core * fold + i % fold

        @pl.when(jnp.logical_not(q_own & (py == y)))
        def _():
            greet((py * nx + x, z * 2 + side))

    @pl.loop(1, nx)
    def _(ox):
        greet((y * nx + (x + ox) % nx, tensor))

    greet(sibling)
    greet(z_prev)

    own_rows.wait()

    @pl.loop(0, slots)
    def _(offset):
        g_stage[offset] = g_ref[inverse(target(offset))]

    pl.semaphore_wait(
        barrier,
        slots - own.astype(jnp.int32) + half - q_own.astype(jnp.int32) + nx - 1 + 2,
    )

    shard = q_ref.shape[1]
    pieces = PIECES
    piece = shard // pieces
    q_relay = (q_relay_first, q_relay_last)

    def q_span(part):
        return pl.ds(part * piece, piece)

    def q_spot(hh, i, part):
        return q_relay[part].at[hh, i]

    def q_out(i, part):
        return remote(
            q_ref.at[0, q_span(part)], q_spot(side, y_low % fold, part), q_send.at[i, part],
            q_recv.at[side, y_low % fold, part], ((core * half + i) * nx + x, z * 2 + q_core),
        )

    def send_q():
        for part in range(pieces):

            @pl.loop(0, half)
            def _(j):
                i = (y_low + j) % half
                keep = q_own & (i == y_low)

                @pl.when(keep)
                def _():
                    pltpu.make_async_copy(
                        q_ref.at[0, q_span(part)], q_spot(side, y_low % fold, part),
                        q_recv.at[side, y_low % fold, part],
                    ).start()

                @pl.when(jnp.logical_not(keep))
                def _():
                    q_out(i, part).start()

    def p_part(t):
        return p_half.at[pl.ds(pl.multiple_of(t * part, part), part), :]

    def p_stored(which, t):
        return p_ref.at[0, pl.ds(pl.multiple_of(which * half_block + t * part, part), part), :]

    def p_side(t):
        return remote(p_stored(1 - core, t), p_part(t), p_sib.at[t], p_recv.at[t], sibling)

    def p_out(t):
        return remote(p_part(t), p_part(t), p_send.at[t], p_recv.at[t], z_next)

    def p_first(t):
        return remote(p_stored(core, t), p_part(t), p_send.at[t], p_recv.at[t], z_next)

    passes = (hop < nz - 1) & jnp.logical_not(source)

    def send_p():
        @pl.when(source)
        def _():
            @pl.loop(0, chunks)
            def _(t):
                p_first(t).start()
                p_side(t).start()
                pltpu.make_async_copy(p_stored(core, t), p_part(t), p_recv.at[t]).start()

    def pass_p(first, last):
        @pl.loop(first, last)
        def _(t):
            arrived(p_part(t), p_recv.at[t])

            @pl.when(passes)
            def _():
                p_out(t).start()

    def g_out(w):
        return remote(
            g_stage.at[w], g_rows(side, mine), g_send.at[w], g_recv.at[2 * (w % wave_size) + x % 2],
            partner(target(w)),
        )

    def send_g(first, last):
        @pl.loop(first, last)
        def _(w):
            keep = own & (target(w) == mine)

            @pl.when(keep)
            def _():
                pltpu.make_async_copy(g_stage.at[w], g_rows(side, mine), g_recv.at[x % 2]).start()

            @pl.when(jnp.logical_not(keep))
            def _():
                g_out(w).start()

    def q_part(which, column, part):
        return q_full.at[which, :, column, q_span(part)]

    def x_out(ox, part):
        return remote(
            q_stage.at[ox, :, q_span(part)], q_part(core, x, part), x_send.at[ox, part], x_recv.at[ox, part],
            (y * nx + (x + ox) % nx, tensor),
        )

    def q_forward(ox, part):
        spot = q_part(core, (x - ox + nx) % nx, part)
        return remote(spot, spot, qf_send.at[ox, part], qf_recv.at[ox, part], sibling)

    def turn_q(part):
        @pl.loop(0, half)
        def _(i):
            arrived(q_spot(i // fold, i % fold, part), q_recv.at[i // fold, i % fold, part])

        @pl.loop(1, nx)
        def _(ox):
            q_stage[ox, :, q_span(part)] = q_relay[part][inverse(y_low * nx + (x + ox) % nx) % MATS]
            x_out(ox, part).start()

        q_full[core, :, x, q_span(part)] = q_relay[part][inverse(mine) % MATS]
        q_forward(0, part).start()

    def pass_q():
        for part in range(pieces):

            @pl.loop(1, nx)
            def _(ox):
                arrived(q_part(core, (x - ox + nx) % nx, part), x_recv.at[ox, part])
                q_forward(ox, part).start()

    def take_q():
        for part in range(pieces):

            @pl.loop(0, nx)
            def _(ox):
                arrived(q_part(1 - core, (x - ox + nx) % nx, part), qf_recv.at[ox, part])

    def g_forward(offset):
        piece = g_rows(core, sender(offset))
        return remote(piece, piece, gf_send.at[offset], gf_recv.at[offset], sibling)

    def pass_g(first, last, total):
        def one(t, total):
            pos = sender(t)
            arrived(g_rows(core, pos), g_recv.at[t])
            g_forward(t).start()
            values = g_rows(core, pos)[...].astype(jnp.float32)
            return total + jnp.sum((values * values).reshape(-1, 8, 128), axis=0)

        return lax.fori_loop(first, last, one, total)

    def take_g(first, last):
        @pl.loop(first, last)
        def _(offset):
            arrived(g_rows(1 - core, sender(offset)), gf_recv.at[offset])

    width = 256

    span = rows * nx

    def left_part(which, first, begin, end):
        tops = [
            pl.multiple_of((which * slots + ((y_low - first - i + half) % half) * nx) * rows, span) for i in range(2)
        ]
        left = jnp.concatenate([p_half[:, pl.ds(top, span)] for top in tops], axis=1)

        @pl.loop(0, block // width)
        def _(n):
            cols = pl.ds(pl.multiple_of(n * width, width), width)
            right = jnp.concatenate([g_full[pl.ds(top, span), cols] for top in tops], axis=0)
            value = jnp.dot(left, right, preferred_element_type=jnp.float32)
            if not begin:
                value = z_sum[:, cols] + value
            if end:
                z_buf[:, cols] = value.astype(jnp.bfloat16)
            else:
                z_sum[:, cols] = value

    def right_product():
        def right(n, total):
            cols = pl.ds(pl.multiple_of(n * width, width), width)
            factor = q_full[:, :, :, :, cols].reshape(block, width)
            value = jnp.dot(z_buf[...], factor, preferred_element_type=jnp.float32)
            u_buf[:, cols] = value
            return total + jnp.sum((value * value).reshape(-1, 8, 128), axis=0)

        return lax.fori_loop(0, block // width, right, jnp.zeros((8, 128), jnp.float32))

    def u_out(offset):
        return remote(
            u_stage.at[offset], u_recv.at[mine], u_send.at[offset], u_in.at[offset],
            partner(place(offset, -1)),
        )

    def send_u(graft):
        def scaled(offset):
            first = pl.multiple_of(place(offset, -1) * rows, rows)
            return (u_buf[pl.ds(first, rows), :] * graft).astype(jnp.bfloat16)

        u_stage[0] = scaled(0)

        @pl.when(own)
        def _():
            pltpu.make_async_copy(u_stage.at[0], u_recv.at[mine], u_in.at[0]).start()

        @pl.when(jnp.logical_not(own))
        def _():
            u_out(0).start()

        @pl.loop(1, slots)
        def _(turn):
            offset = (turn + 2 * nx - 1) % (slots - 1) + 1
            u_stage[offset] = scaled(offset)
            u_out(offset).start()

    def sent_g(first, last):
        @pl.loop(first, last)
        def _(w):
            @pl.when(jnp.logical_not(own & (target(w) == mine)))
            def _():
                g_out(w).wait_send()

    def left_g():
        @pl.loop(0, slots)
        def _(offset):
            g_forward(offset).wait_send()

    def left_q():
        for part in range(pieces):

            @pl.loop(0, half)
            def _(i):
                @pl.when(jnp.logical_not(q_own & (i == y_low)))
                def _():
                    q_out(i, part).wait_send()

            @pl.loop(1, nx)
            def _(ox):
                x_out(ox, part).wait_send()

            @pl.loop(0, nx)
            def _(ox):
                q_forward(ox, part).wait_send()

    def left_p():
        @pl.when(source)
        def _():
            @pl.loop(0, chunks)
            def _(t):
                p_side(t).wait_send()

        @pl.when(hop < nz - 1)
        def _():
            @pl.loop(0, chunks)
            def _(t):
                p_out(t).wait_send()

    def take_u():
        @pl.loop(0, slots)
        def _(offset):
            arrived(u_recv.at[place(offset, 1)], u_in.at[offset])

        @pl.when(jnp.logical_not(own))
        def _():
            u_out(0).wait_send()

        @pl.loop(1, slots)
        def _(offset):
            u_out(offset).wait_send()

    send_q()
    send_p()
    send_g(0, wave_size // 2)
    first_cut = jnp.clip((9 - 3 * hop) * 4 // 3 * chunks // 16, 0, chunks)
    second_cut = jnp.clip((15 - 3 * hop) * 4 // 3 * chunks // 16, first_cut, chunks)
    pass_p(0, first_cut)
    turn_q(0)
    send_g(wave_size // 2, wave_size)
    pass_p(first_cut, second_cut)
    turn_q(1)
    send_g(wave_size, slots)
    pass_p(second_cut, chunks)
    zero = jnp.zeros((8, 128), jnp.float32)
    middle = slots // 2
    part_sum = pass_g(0, middle, zero)
    left_part(core, 0, True, False)
    pass_q()
    take_g(0, middle)
    left_part(1 - core, 0, False, False)
    sums[0] = pass_g(middle, slots, part_sum)
    left_part(core, 2, False, False)
    take_g(middle, slots)
    left_part(1 - core, 2, False, True)
    take_q()
    sums[1] = right_product()
    exchange = remote(sums, sums_in, s_sem.at[0], s_sem.at[1], sibling)
    exchange.start()
    exchange.wait()
    graft = jnp.sqrt(jnp.sum(sums[0] + sums_in[0]) / (jnp.sum(sums[1] + sums_in[1]) + 1e-06))
    send_u(graft)
    sent_g(0, slots)
    left_g()
    left_q()
    left_p()
    take_u()

    @pl.loop(0, slots)
    def _(k):
        o_ref[k] = u_recv[slot_ref[k]]


def local(nx, ny, nz, grads, left_slot, left_roots, right_roots):
    slots, rows, block = grads.shape
    half = ny // 2
    fold = half // 2
    chunks = slots
    pieces = PIECES
    shard = right_roots.shape[1]
    bf16, f32 = jnp.bfloat16, jnp.float32
    dma = pltpu.SemaphoreType.DMA
    vmem = pl.BlockSpec(memory_space=pltpu.VMEM)
    hbm = pl.BlockSpec(memory_space=pl.ANY)
    return pl.pallas_call(
        functools.partial(kernel, nx, ny, nz, chunks),
        out_shape=jax.ShapeDtypeStruct(grads.shape, bf16),
        in_specs=[pl.BlockSpec(memory_space=pltpu.SMEM), hbm, hbm, hbm],
        out_specs=vmem,
        scratch_shapes=[
            pltpu.VMEM((slots, rows, block), bf16),
            pltpu.VMEM((slots, rows, block), bf16),
            pltpu.VMEM((block, block), bf16),
            pltpu.VMEM((block // 2, block), bf16),
            pltpu.VMEM((MATS, fold, shard // pieces, block), bf16),
            pltpu.VMEM((MATS, fold, shard // pieces, block), bf16),
            pltpu.VMEM((nx, fold, shard, block), bf16),
            pltpu.VMEM((2, fold, nx, shard, block), bf16),
            pltpu.VMEM((block // 2, block), f32),
            pltpu.VMEM((block // 2, block), bf16),
            pltpu.VMEM((block // 2, block), f32),
            pltpu.VMEM((slots, rows, block), bf16),
            pltpu.VMEM((slots, rows, block), bf16),
            pltpu.VMEM((2, 8, 128), f32),
            pltpu.VMEM((2, 8, 128), f32),
            dma((slots,)), dma((slots,)), dma((slots,)), dma((slots,)),
            dma((chunks,)), dma((chunks,)), dma((chunks,)),
            dma((half, pieces)), dma((MATS, fold, pieces)),
            dma((nx, pieces)), dma((nx, pieces)), dma((nx, pieces)), dma((nx, pieces)),
            dma((2,)),
            dma((slots,)), dma((slots,)), dma,
        ],
        compiler_params=pltpu.CompilerParams(
            collective_id=0, has_side_effects=True, vmem_limit_bytes=60 * MIB
        ),
        cost_estimate=pl.CostEstimate(
            flops=2 * block * block * block, bytes_accessed=16 * MIB, transcendentals=0
        ),
        name="precondition",
    )(left_slot, grads, left_roots, right_roots)


def solution(mesh):
    nx = CHIPS_X
    ny = mesh.shape["dp"] // nx
    nz = mesh.shape["tensor"] // 2
    in_specs = (P(None, "dp", "tensor"), P(), P("tensor", None, None), P("tensor", "dp", None))
    out_specs = P(None, "dp", "tensor")
    return jax.shard_map(
        functools.partial(local, nx, ny, nz), mesh=mesh, in_specs=in_specs, out_specs=out_specs, check_vma=False
    )
```

```python
import functools

import jax
import jax.numpy as jnp
from jax import lax
from jax.experimental import pallas as pl
from jax.experimental.pallas import tpu as pltpu
from jax.sharding import PartitionSpec as P

MESH = pl.DeviceIdType.MESH
CHIPS_X = 4
MATS = 2
MIB = 1 << 20
PIECES = 2


def kernel(
    nx, ny, nz, chunks,
    slot_ref, g_hbm, p_ref, q_ref, o_ref,
    g_ref, g_stage, g_full, p_half, q_relay_first, q_relay_last, q_stage, q_full, z_sum, z_buf, u_buf, u_stage, u_recv, sums, sums_in,
    g_send, g_recv, gf_send, gf_recv, p_send, p_sib, p_recv, q_send, q_recv, x_send, x_recv,
    qf_send, qf_recv, s_sem, u_send, u_in, in_sem,
):
    half = ny // 2
    fold = half // 2
    slots = half * nx
    rows = g_ref.shape[1]
    block = g_ref.shape[2]
    half_block = block // 2
    part = half_block // chunks
    dp = lax.axis_index("dp")
    tensor = lax.axis_index("tensor")
    y, x = dp // nx, dp % nx
    z, core = tensor // 2, tensor % 2
    side, y_low = y // half, y % half
    mine = y_low * nx + x
    own = core == side
    sibling = (dp, z * 2 + 1 - core)
    step = 1 - 2 * core
    z_next = (dp, ((z + step + nz) % nz) * 2 + core)
    z_prev = (dp, ((z - step + nz) % nz) * 2 + core)
    hop = ((z - mine // 2) * step + nz) % nz
    source = (hop == 0) & (core == mine % 2)
    q_core = y_low // fold
    q_own = own & (q_core == core)

    def inverse(slot):
        found = 0
        for k in range(slots):
            found = jnp.where(slot_ref[k] == slot, k, found)
        return found

    def place(offset, sign):
        py = (y_low + sign * (offset // nx) + half) % half
        px = (x + sign * (offset % nx) + nx) % nx
        return py * nx + px

    pairs = nx // 2
    wave_size = slots // 2

    def target(w):
        wave, i = w // wave_size, w % wave_size
        py = (y_low + i // pairs + half // 2) % half
        px = 2 * ((x // 2 + i) % pairs) + (wave + py) % 2
        return py * nx + px

    def sender(e):
        i = e // 2
        sy = (y_low - i // pairs + half + half // 2) % half
        sx = 2 * ((x // 2 - i % pairs + pairs) % pairs) + e % 2
        return sy * nx + sx

    def partner(pos):
        return (core * slots + pos, z * 2 + side)

    def remote(src, dst, send, recv, device):
        return pltpu.make_async_remote_copy(
            src_ref=src, dst_ref=dst, send_sem=send, recv_sem=recv, device_id=device, device_id_type=MESH
        )

    def arrived(dst, sem):
        pltpu.make_async_copy(dst, dst, sem).wait()

    def g_rows(which, pos):
        return g_full.at[pl.ds(pl.multiple_of((which * slots + pos) * rows, rows), rows), :]

    own_rows = pltpu.make_async_copy(g_hbm, g_ref, in_sem)
    own_rows.start()

    barrier = pltpu.get_barrier_semaphore()

    def greet(device):
        pl.semaphore_signal(barrier, inc=1, device_id=device, device_id_type=MESH)

    @pl.loop(1, slots)
    def _(offset):
        greet(partner(place(offset, 1)))

    @pl.when(jnp.logical_not(own))
    def _():
        greet(partner(mine))

    @pl.loop(0, half)
    def _(i):
        py = (i // fold) * half + core * fold + i % fold

        @pl.when(jnp.logical_not(q_own & (py == y)))
        def _():
            greet((py * nx + x, z * 2 + side))

    @pl.loop(1, nx)
    def _(ox):
        greet((y * nx + (x + ox) % nx, tensor))

    greet(sibling)
    greet(z_prev)

    own_rows.wait()

    @pl.loop(0, slots)
    def _(offset):
        g_stage[offset] = g_ref[inverse(target(offset))]

    pl.semaphore_wait(
        barrier,
        slots - own.astype(jnp.int32) + half - q_own.astype(jnp.int32) + nx - 1 + 2,
    )

    shard = q_ref.shape[1]
    pieces = PIECES
    piece = shard // pieces
    q_relay = (q_relay_first, q_relay_last)

    def q_span(part):
        return pl.ds(part * piece, piece)

    def q_spot(hh, i, part):
        return q_relay[part].at[hh, i]

    def q_out(i, part):
        return remote(
            q_ref.at[0, q_span(part)], q_spot(side, y_low % fold, part), q_send.at[i, part],
            q_recv.at[side, y_low % fold, part], ((core * half + i) * nx + x, z * 2 + q_core),
        )

    def send_q():
        for part in range(pieces):

            @pl.loop(0, half)
            def _(j):
                i = (y_low + j) % half
                keep = q_own & (i == y_low)

                @pl.when(keep)
                def _():
                    pltpu.make_async_copy(
                        q_ref.at[0, q_span(part)], q_spot(side, y_low % fold, part),
                        q_recv.at[side, y_low % fold, part],
                    ).start()

                @pl.when(jnp.logical_not(keep))
                def _():
                    q_out(i, part).start()

    def p_part(t):
        return p_half.at[pl.ds(pl.multiple_of(t * part, part), part), :]

    def p_stored(which, t):
        return p_ref.at[0, pl.ds(pl.multiple_of(which * half_block + t * part, part), part), :]

    def p_side(t):
        return remote(p_stored(1 - core, t), p_part(t), p_sib.at[t], p_recv.at[t], sibling)

    def p_out(t):
        return remote(p_part(t), p_part(t), p_send.at[t], p_recv.at[t], z_next)

    def p_first(t):
        return remote(p_stored(core, t), p_part(t), p_send.at[t], p_recv.at[t], z_next)

    passes = (hop < nz - 1) & jnp.logical_not(source)

    def send_p():
        @pl.when(source)
        def _():
            @pl.loop(0, chunks)
            def _(t):
                p_first(t).start()
                p_side(t).start()
                pltpu.make_async_copy(p_stored(core, t), p_part(t), p_recv.at[t]).start()

    def pass_p(first, last):
        @pl.loop(first, last)
        def _(t):
            arrived(p_part(t), p_recv.at[t])

            @pl.when(passes)
            def _():
                p_out(t).start()

    def g_out(w):
        return remote(
            g_stage.at[w], g_rows(side, mine), g_send.at[w], g_recv.at[2 * (w % wave_size) + x % 2],
            partner(target(w)),
        )

    def send_g(first, last):
        @pl.loop(first, last)
        def _(w):
            keep = own & (target(w) == mine)

            @pl.when(keep)
            def _():
                pltpu.make_async_copy(g_stage.at[w], g_rows(side, mine), g_recv.at[2 * (w % wave_size) + x % 2]).start()

            @pl.when(jnp.logical_not(keep))
            def _():
                g_out(w).start()

    def q_part(which, column, part):
        return q_full.at[which, :, column, q_span(part)]

    def x_out(ox, part):
        return remote(
            q_stage.at[ox, :, q_span(part)], q_part(core, x, part), x_send.at[ox, part], x_recv.at[ox, part],
            (y * nx + (x + ox) % nx, tensor),
        )

    def q_forward(ox, part):
        spot = q_part(core, (x - ox + nx) % nx, part)
        return remote(spot, spot, qf_send.at[ox, part], qf_recv.at[ox, part], sibling)

    def turn_q(part):
        @pl.loop(0, half)
        def _(i):
            arrived(q_spot(i // fold, i % fold, part), q_recv.at[i // fold, i % fold, part])

        @pl.loop(1, nx)
        def _(ox):
            q_stage[ox, :, q_span(part)] = q_relay[part][inverse(y_low * nx + (x + ox) % nx) % MATS]
            x_out(ox, part).start()

        q_full[core, :, x, q_span(part)] = q_relay[part][inverse(mine) % MATS]
        q_forward(0, part).start()

    def pass_q():
        for part in range(pieces):

            @pl.loop(1, nx)
            def _(ox):
                arrived(q_part(core, (x - ox + nx) % nx, part), x_recv.at[ox, part])
                q_forward(ox, part).start()

    def take_q():
        for part in range(pieces):

            @pl.loop(0, nx)
            def _(ox):
                arrived(q_part(1 - core, (x - ox + nx) % nx, part), qf_recv.at[ox, part])

    def g_forward(offset):
        piece = g_rows(core, sender(offset))
        return remote(piece, piece, gf_send.at[offset], gf_recv.at[offset], sibling)

    def pass_g(first, last, total):
        def one(t, total):
            pos = sender(t)
            arrived(g_rows(core, pos), g_recv.at[t])
            g_forward(t).start()
            values = g_rows(core, pos)[...].astype(jnp.float32)
            return total + jnp.sum((values * values).reshape(-1, 8, 128), axis=0)

        return lax.fori_loop(first, last, one, total)

    def take_g(first, last):
        @pl.loop(first, last)
        def _(offset):
            arrived(g_rows(1 - core, sender(offset)), gf_recv.at[offset])

    width = 256

    span = rows * nx

    def left_part(which, first, begin, end):
        tops = [
            pl.multiple_of((which * slots + ((y_low - first - i + half + half // 2) % half) * nx) * rows, span) for i in range(2)
        ]
        left = jnp.concatenate([p_half[:, pl.ds(top, span)] for top in tops], axis=1)

        @pl.loop(0, block // width)
        def _(n):
            cols = pl.ds(pl.multiple_of(n * width, width), width)
            right = jnp.concatenate([g_full[pl.ds(top, span), cols] for top in tops], axis=0)
            value = jnp.dot(left, right, preferred_element_type=jnp.float32)
            if not begin:
                value = z_sum[:, cols] + value
            if end:
                z_buf[:, cols] = value.astype(jnp.bfloat16)
            else:
                z_sum[:, cols] = value

    def right_product():
        def right(n, total):
            cols = pl.ds(pl.multiple_of(n * width, width), width)
            factor = q_full[:, :, :, :, cols].reshape(block, width)
            value = jnp.dot(z_buf[...], factor, preferred_element_type=jnp.float32)
            u_buf[:, cols] = value
            return total + jnp.sum((value * value).reshape(-1, 8, 128), axis=0)

        return lax.fori_loop(0, block // width, right, jnp.zeros((8, 128), jnp.float32))

    def u_out(offset):
        return remote(
            u_stage.at[offset], u_recv.at[mine], u_send.at[offset], u_in.at[offset],
            partner(place(offset, -1)),
        )

    def send_u(graft):
        def scaled(offset):
            first = pl.multiple_of(place(offset, -1) * rows, rows)
            return (u_buf[pl.ds(first, rows), :] * graft).astype(jnp.bfloat16)

        u_stage[0] = scaled(0)

        @pl.when(own)
        def _():
            pltpu.make_async_copy(u_stage.at[0], u_recv.at[mine], u_in.at[0]).start()

        @pl.when(jnp.logical_not(own))
        def _():
            u_out(0).start()

        @pl.loop(1, slots)
        def _(turn):
            offset = (turn + 2 * nx - 1) % (slots - 1) + 1
            u_stage[offset] = scaled(offset)
            u_out(offset).start()

    def sent_g(first, last):
        @pl.loop(first, last)
        def _(w):
            @pl.when(jnp.logical_not(own & (target(w) == mine)))
            def _():
                g_out(w).wait_send()

    def left_g():
        @pl.loop(0, slots)
        def _(offset):
            g_forward(offset).wait_send()

    def left_q():
        for part in range(pieces):

            @pl.loop(0, half)
            def _(i):
                @pl.when(jnp.logical_not(q_own & (i == y_low)))
                def _():
                    q_out(i, part).wait_send()

            @pl.loop(1, nx)
            def _(ox):
                x_out(ox, part).wait_send()

            @pl.loop(0, nx)
            def _(ox):
                q_forward(ox, part).wait_send()

    def left_p():
        @pl.when(source)
        def _():
            @pl.loop(0, chunks)
            def _(t):
                p_side(t).wait_send()

        @pl.when(hop < nz - 1)
        def _():
            @pl.loop(0, chunks)
            def _(t):
                p_out(t).wait_send()

    def take_u():
        @pl.loop(0, slots)
        def _(offset):
            arrived(u_recv.at[place(offset, 1)], u_in.at[offset])

        @pl.when(jnp.logical_not(own))
        def _():
            u_out(0).wait_send()

        @pl.loop(1, slots)
        def _(offset):
            u_out(offset).wait_send()

    send_q()
    send_p()
    send_g(0, wave_size // 2)
    first_cut = jnp.clip((9 - 3 * hop) * 4 // 3 * chunks // 16, 0, chunks)
    second_cut = jnp.clip((15 - 3 * hop) * 4 // 3 * chunks // 16, first_cut, chunks)
    pass_p(0, first_cut)
    turn_q(0)
    send_g(wave_size // 2, wave_size)
    pass_p(first_cut, second_cut)
    turn_q(1)
    send_g(wave_size, slots)
    pass_p(second_cut, chunks)
    zero = jnp.zeros((8, 128), jnp.float32)
    middle = slots // 2
    part_sum = pass_g(0, middle, zero)
    left_part(core, 0, True, False)
    pass_q()
    take_g(0, middle)
    left_part(1 - core, 0, False, False)
    sums[0] = pass_g(middle, slots, part_sum)
    left_part(core, 2, False, False)
    take_g(middle, slots)
    left_part(1 - core, 2, False, True)
    take_q()
    sums[1] = right_product()
    exchange = remote(sums, sums_in, s_sem.at[0], s_sem.at[1], sibling)
    exchange.start()
    exchange.wait()
    graft = jnp.sqrt(jnp.sum(sums[0] + sums_in[0]) / (jnp.sum(sums[1] + sums_in[1]) + 1e-06))
    send_u(graft)
    sent_g(0, slots)
    left_g()
    left_q()
    left_p()
    take_u()

    @pl.loop(0, slots)
    def _(k):
        o_ref[k] = u_recv[slot_ref[k]]


def local(nx, ny, nz, grads, left_slot, left_roots, right_roots):
    slots, rows, block = grads.shape
    half = ny // 2
    fold = half // 2
    chunks = slots
    pieces = PIECES
    shard = right_roots.shape[1]
    bf16, f32 = jnp.bfloat16, jnp.float32
    dma = pltpu.SemaphoreType.DMA
    vmem = pl.BlockSpec(memory_space=pltpu.VMEM)
    hbm = pl.BlockSpec(memory_space=pl.ANY)
    return pl.pallas_call(
        functools.partial(kernel, nx, ny, nz, chunks),
        out_shape=jax.ShapeDtypeStruct(grads.shape, bf16),
        in_specs=[pl.BlockSpec(memory_space=pltpu.SMEM), hbm, hbm, hbm],
        out_specs=vmem,
        scratch_shapes=[
            pltpu.VMEM((slots, rows, block), bf16),
            pltpu.VMEM((slots, rows, block), bf16),
            pltpu.VMEM((block, block), bf16),
            pltpu.VMEM((block // 2, block), bf16),
            pltpu.VMEM((MATS, fold, shard // pieces, block), bf16),
            pltpu.VMEM((MATS, fold, shard // pieces, block), bf16),
            pltpu.VMEM((nx, fold, shard, block), bf16),
            pltpu.VMEM((2, fold, nx, shard, block), bf16),
            pltpu.VMEM((block // 2, block), f32),
            pltpu.VMEM((block // 2, block), bf16),
            pltpu.VMEM((block // 2, block), f32),
            pltpu.VMEM((slots, rows, block), bf16),
            pltpu.VMEM((slots, rows, block), bf16),
            pltpu.VMEM((2, 8, 128), f32),
            pltpu.VMEM((2, 8, 128), f32),
            dma((slots,)), dma((slots,)), dma((slots,)), dma((slots,)),
            dma((chunks,)), dma((chunks,)), dma((chunks,)),
            dma((half, pieces)), dma((MATS, fold, pieces)),
            dma((nx, pieces)), dma((nx, pieces)), dma((nx, pieces)), dma((nx, pieces)),
            dma((2,)),
            dma((slots,)), dma((slots,)), dma,
        ],
        compiler_params=pltpu.CompilerParams(
            collective_id=0, has_side_effects=True, vmem_limit_bytes=60 * MIB
        ),
        cost_estimate=pl.CostEstimate(
            flops=2 * block * block * block, bytes_accessed=16 * MIB, transcendentals=0
        ),
        name="precondition",
    )(left_slot, grads, left_roots, right_roots)


def solution(mesh):
    nx = CHIPS_X
    ny = mesh.shape["dp"] // nx
    nz = mesh.shape["tensor"] // 2
    in_specs = (P(None, "dp", "tensor"), P(), P("tensor", None, None), P("tensor", "dp", None))
    out_specs = P(None, "dp", "tensor")
    return jax.shard_map(
        functools.partial(local, nx, ny, nz), mesh=mesh, in_specs=in_specs, out_specs=out_specs, check_vma=False
    )
```
